32 devices in a mesh: dp: 16 (over z, y, core), mp: 2 (over x).
Axes of the slice: x: 2, y: 2, z: 4, core: 2. Of those that a mesh axis runs over, the one named last changes fastest.
Arguments:
- context: bfloat16 [16384, 2048], P('dp', 'mp'), may hold values from -6 to 6
- cotangent: bfloat16 [16384, 4096], P(('dp', 'mp')), may hold values from -6 to 6
- lengths: int32 [512], P(('dp', 'mp')), may hold values from 1 to 32, as said below
- weight: float32 [2048, 4096], P('mp', 'dp'), may hold values from -0.125 to 0.125
- row_stat: float32 [2048], P('mp'), may hold values from 0.01 to 0.3
- col_stat: float32 [4096], P('dp'), may hold values from 0.01 to 0.3
Outputs:
- context_grad: bfloat16 [16384, 2048], P('dp', 'mp')
- update: float32 [2048, 4096], P('mp', 'dp')
- row_new: float32 [2048], P('mp')
- col_new: float32 [4096], P('dp')
The draws below stay inside these ranges and needn't reach their ends.
Inputs may be any that keep to these rules, and one draw needn't show every extreme that they name: The first lengths entry of each sequence's 32 slots are real tokens, the rest padding.
All inputs are finite; a program needn't handle non-finite values.
Results may differ from the reference program's by a relative error of at most 0.0049.
Values may be sent and summed in bfloat16 or wider, within the bound.
A program may use at most 128 MiB of HBM per device.

```python
import math
import jax
import jax.numpy as jnp
from jax import lax

D = 4096
TGT_LEN = 32
INNER = 2048
TOKENS = 16384
SEQS = 512
N_DP = 16


def draw_lengths(key, part):
    values = jax.random.randint(key, (SEQS,), 1, TGT_LEN + 1).astype(jnp.int32)
    return values.at[0].set(TGT_LEN)


def spiked(array, key, source, target, shards_of, factor):
    owner, partner = [(jnp.arange(array.shape[dim]) // (array.shape[dim] // shards_of)).reshape([-1 if axis == dim else 1 for axis in range(array.ndim)]) for dim in (source, target)]
    chosen = jax.random.permutation(key, shards_of)[partner]
    strong = (owner == chosen) | (owner == (partner + shards_of // 2) % shards_of)
    return jnp.where(strong, factor * array, array)


def block_levels(rng, shape, cuts, least, top_value):
    loudness, own = 1.0, jax.random.fold_in(rng, 6)
    for dim, parts in cuts:
        heights = jnp.exp(jax.random.uniform(jax.random.fold_in(own, dim), (parts,), jnp.float32, least / len(cuts), top_value / len(cuts)))
        loudness = loudness * jnp.repeat(heights, shape[dim] // parts).reshape([-1 if axis == dim else 1 for axis in range(len(shape))])
    return loudness


def normal_values(own_key, dims, width, most, split=(), held_as=jnp.bfloat16):
    drawn = width * jax.random.normal(own_key, dims, jnp.float32)
    if split:
        drawn = drawn * block_levels(own_key, dims, split, -0.22, 0.18)
    return jnp.clip(drawn, -most, most).astype(held_as)


def gaussian_with(rng, extent, deviation, bound, pieces, heavy, kind=jnp.bfloat16):
    values = deviation * jax.random.normal(rng, extent, jnp.float32)
    if pieces:
        values = values * block_levels(rng, extent, pieces, -0.22, 0.18)
    return jnp.clip(spiked(values, jax.random.fold_in(rng, 3), *heavy), -bound, bound).astype(kind)


def setup_inputs(seed: int = 0) -> dict:
    splits = jax.random.split(jax.random.key(seed), 7)
    return {
        "context": normal_values(splits[0], (TOKENS, INNER), 1.0, 6.0, ((0, 16), (1, 2))),
        "cotangent": gaussian_with(splits[1], (TOKENS, D), 1.0, 6.0, ((0, 32),), (0, 1, 32, 2.75)),
        "lengths": draw_lengths(jax.random.fold_in(splits[6], 71), 0),
        "weight": normal_values(splits[3], (INNER, D), INNER ** -0.5, 0.125, ((0, 2), (1, 16)), jnp.float32),
        "row_stat": jnp.clip(jnp.exp(math.log(0.3) - 3.4011974 * jax.random.uniform(splits[4], (INNER,), jnp.float32) ** block_levels(splits[4], (INNER,), ((0, 2),), -0.2, 0.2)), 0.01, 0.3),
        "col_stat": jnp.clip(jnp.exp(math.log(0.3) - 3.4011974 * jax.random.uniform(splits[5], (D,), jnp.float32) ** block_levels(splits[5], (D,), ((0, 16),), -0.2, 0.2)), 0.01, 0.3),
    }


decay_rate = 0.9
square_eps = 1e-30

def reference(context, cotangent, lengths, weight, row_stat, col_stat):
    seq_count = lengths.shape[0]
    position = jnp.arange(TGT_LEN, dtype=jnp.int32)
    inside = position[None, :] < lengths[:, None]
    shaped = cotangent.reshape(seq_count, TGT_LEN, D)
    masked = jnp.where(inside[:, :, None], shaped, jnp.zeros((), cotangent.dtype)).reshape(-1, D)
    weight_b = weight.astype(jnp.bfloat16)
    context_grad = jnp.dot(masked, weight_b.T, preferred_element_type=jnp.float32).astype(jnp.bfloat16)
    grad = jnp.dot(context.T, masked, preferred_element_type=jnp.float32) / N_DP
    square = grad * grad + square_eps
    row_new = decay_rate * row_stat + (1.0 - decay_rate) * lax.optimization_barrier(jnp.mean(square, axis=1))
    col_new = decay_rate * col_stat + (1.0 - decay_rate) * lax.optimization_barrier(jnp.mean(square, axis=0))
    raw_update = grad / jnp.sqrt(row_new[:, None] * col_new[None, :])
    update_rms = jnp.sqrt(jnp.mean(raw_update * raw_update))
    update = raw_update / jnp.maximum(1.0, update_rms)
    return (context_grad, update, row_new, col_new)
```

```python
import functools
import jax
import jax.numpy as jnp
from jax import lax
from jax.experimental import pallas as pl
from jax.experimental.pallas import tpu as pltpu
from jax.sharding import PartitionSpec as P

decay_rate = 0.9
square_eps = 1e-30
LANES = 128
TILE = 256
WINDOW = 3
MESH = pl.DeviceIdType.MESH


def low_bit(r, n):
    return r & -r if r else n


def flip(me, r):
    out = me
    bit = 1
    while bit <= r:
        if r & bit:
            out = out + bit * (1 - 2 * (lax.rem(lax.div(me, bit), 2)))
        bit *= 2
    return out


def schedule(n):
    half = n // 2
    first = list(range(n - 2, half - 1, -2))
    second = sorted(range(0, half, 2), key=lambda r: (low_bit(r, n), -r))
    order = [b for r in first + second for b in (r + 1, r)]
    pos = {r: k for k, r in enumerate(order)}
    after = {}
    for r in sorted(range(2, n, 2), key=lambda r: low_bit(r, n)):
        when, bit = pos[r], 2
        while bit < low_bit(r, n):
            when = max(when, after[r + bit] + 3)
            bit *= 2
        after[r] = min(when, n - 2)
    return order, after


def weight_arrivals(n):
    return sorted(range(2, n, 2), key=lambda r: (bin(r).count("1") + (n // low_bit(r, n)).bit_length(), r))


def kernel(n, mask_ref, cot_ref, ctx_ref, w_ref, row_ref, col_ref,
           cg_ref, up_ref, rown_ref, coln_ref,
           ctx_t, g_all, w_all, inbox, outbox, kept, cg_acc, rv, cx, sx,
           x_send, x_recv, w_send, w_recv, r_send, r_recv, v_send, v_recv, p_send, p_recv):
    me, mp = lax.axis_index("dp"), lax.axis_index("mp")
    other = 1 - mp
    t, width = cot_ref.shape
    heads, cols = w_ref.shape
    groups = heads // LANES
    own_rows = pl.ds(pl.multiple_of(mp * t, t), t)

    barrier = pltpu.get_barrier_semaphore()
    for q in range(1, n):
        pl.semaphore_signal(barrier, inc=1, device_id=(flip(me, q), mp), device_id_type=MESH)
    pl.semaphore_signal(barrier, inc=1, device_id=(me, other), device_id_type=MESH)

    order, after = schedule(n)

    def mask_block(r):
        columns = pl.ds(pl.multiple_of(flip(me, r) * cols, cols), cols)
        m = mask_ref[...]
        m = jnp.concatenate([m] * (cols // LANES), axis=1)
        g_all[r, own_rows, :] = cot_ref[:, columns] * m

    w_all[0] = w_ref[...].astype(jnp.bfloat16)
    for r in order[:WINDOW]:
        mask_block(r)
    pl.semaphore_wait(barrier, n)

    x_copy = {}
    for r in order:
        x_copy[r] = pltpu.make_async_remote_copy(
            src_ref=g_all.at[r, own_rows, :], dst_ref=g_all.at[r, own_rows, :],
            send_sem=x_send.at[r], recv_sem=x_recv.at[r],
            device_id=(me, other), device_id_type=MESH)
    x_in = {
        r: pltpu.make_async_remote_copy(
            src_ref=g_all.at[r, own_rows, :],
            dst_ref=g_all.at[r, pl.ds(pl.multiple_of(other * t, t), t), :],
            send_sem=x_send.at[r], recv_sem=x_recv.at[r],
            device_id=(me, other), device_id_type=MESH)
        for r in order
    }
    for r in order[:WINDOW]:
        x_copy[r].start()

    w_copies = []

    def weight_send(r):
        bit = low_bit(r, n) // 2
        while bit >= 1:
            copy = pltpu.make_async_remote_copy(
                src_ref=w_all.at[r], dst_ref=w_all.at[r ^ bit],
                send_sem=w_send.at[len(w_copies)], recv_sem=w_recv.at[r ^ bit],
                device_id=(flip(me, bit), mp), device_id_type=MESH)
            copy.start()
            w_copies.append(copy)
            bit //= 2

    def weight_wait(r):
        pltpu.make_async_remote_copy(
            src_ref=w_all.at[0], dst_ref=w_all.at[r],
            send_sem=w_send.at[0], recv_sem=w_recv.at[r],
            device_id=(flip(me, 1), mp), device_id_type=MESH).wait_recv()

    weight_send(0)
    for r in order[WINDOW:]:
        mask_block(r)

    tokens = 2 * t
    for i in range(tokens // TILE):
        for j in range(heads // TILE):
            ctx_t[j * TILE:(j + 1) * TILE, i * TILE:(i + 1) * TILE] = ctx_ref[
                i * TILE:(i + 1) * TILE, j * TILE:(j + 1) * TILE].T

    def reduce_copy(r):
        return pltpu.make_async_remote_copy(
            src_ref=outbox.at[r - 1], dst_ref=inbox.at[r - 1],
            send_sem=r_send.at[r], recv_sem=r_recv.at[r],
            device_id=(flip(me, low_bit(r, n)), mp), device_id_type=MESH)

    r_copy = {r: reduce_copy(r) for r in range(1, n)}

    def weight_grad(r):
        @pl.loop(0, heads // TILE)
        def _(i):
            rows = pl.ds(pl.multiple_of(i * TILE, TILE), TILE)
            term = jnp.dot(ctx_t[rows, :], g_all[r], preferred_element_type=jnp.float32)
            if r % 2:
                outbox[r - 1, rows, :] = term.astype(jnp.bfloat16)
            else:
                kept[r // 2, rows, :] = term
        if r % 2:
            r_copy[r].start()

    def incoming(r):
        out, bit = [], 1
        while bit < low_bit(r, n):
            out.append(r + bit)
            bit *= 2
        return out

    def pass_on(r):
        for q in incoming(r):
            r_copy[q].wait_recv()

        @pl.loop(0, heads // TILE)
        def _(i):
            rows = pl.ds(pl.multiple_of(i * TILE, TILE), TILE)
            total = kept[r // 2, rows, :]
            for q in incoming(r):
                total = total + inbox[q - 1, rows, :].astype(jnp.float32)
            outbox[r - 1, rows, :] = total.astype(jnp.bfloat16)
        r_copy[r].start()

    def context_grad(blocks, first, last):
        @pl.loop(0, tokens // TILE)
        def _(i):
            rows = pl.ds(pl.multiple_of(i * TILE, TILE), TILE)
            total = None if first else cg_acc[rows, :]
            for r in blocks:
                term = lax.dot_general(g_all[r, rows, :], w_all[r], (((1,), (1,)), ((), ())),
                                       preferred_element_type=jnp.float32)
                total = term if total is None else total + term
            if last:
                cg_ref[rows, :] = total.astype(jnp.bfloat16)
            else:
                cg_acc[rows, :] = total

    arrivals = weight_arrivals(n)
    w_step = {}
    for k, r in enumerate(arrivals):
        w_step.setdefault(min(1 + (k * (n // 2 - 2)) // max(len(arrivals) - 1, 1), n - 1), []).append(r)
    quarter = n // 4
    cg_step = {n // 2 + 1: 0, n // 2 + 3: 1, 3 * n // 4 + 1: 2}
    w_seen = set(range(0, 1))

    for k, r in enumerate(order):
        x_in[r].wait_recv()
        if k + WINDOW < n:
            x_copy[r].wait_send()
            x_copy[order[k + WINDOW]].start()
        weight_grad(r)
        for q in w_step.get(k, []):
            weight_wait(q)
            w_seen.add(q)
            weight_send(q)
        for q in order:
            if after.get(q) == k:
                pass_on(q)
        if k in cg_step:
            blocks = order[cg_step[k] * quarter:(cg_step[k] + 1) * quarter]
            for q in blocks:
                if q not in w_seen:
                    weight_wait(q)
                    w_seen.add(q)
            context_grad(blocks, cg_step[k] == 0, False)

    for q in incoming(0):
        r_copy[q].wait_recv()
    col_part = jnp.zeros((1, cols), jnp.float32)

    def row_sums(values, base, i):
        folded = values[:, :LANES]
        for c in range(LANES, cols, LANES):
            folded = folded + values[:, c:c + LANES]
        line = jnp.sum(folded.T, axis=0, keepdims=True)
        for c in range(TILE // LANES):
            at = base + i * (TILE // LANES) + c
            rv[0, at:at + 1, :] = line[:, c * LANES:(c + 1) * LANES]

    for i in range(heads // TILE):
        rows = slice(i * TILE, (i + 1) * TILE)
        total = kept[0, rows, :]
        for q in incoming(0):
            total = total + inbox[q - 1, rows, :].astype(jnp.float32)
        grad = total / n
        kept[0, rows, :] = grad
        square = grad * grad + square_eps
        col_part = col_part + jnp.sum(square, axis=0, keepdims=True)
        row_sums(square, 0, i)
    cx[0] = jnp.broadcast_to(col_part, (8, cols))
    col_copy = pltpu.make_async_remote_copy(
        src_ref=cx.at[0], dst_ref=cx.at[1], send_sem=p_send.at[0], recv_sem=p_recv.at[0],
        device_id=(me, other), device_id_type=MESH)
    col_copy.start()
    last = order[3 * quarter:]
    for q in last:
        if q not in w_seen:
            weight_wait(q)
            w_seen.add(q)
    context_grad(last[:len(last) // 2], False, False)
    col_copy.wait_recv()
    col_new = decay_rate * col_ref[...] + (1.0 - decay_rate) * (
        (cx[0, 0:1, :] + cx[1, 0:1, :]) / (2 * heads))
    coln_ref[...] = col_new
    inv_col = 1.0 / col_new
    for i in range(heads // TILE):
        grad = kept[0, i * TILE:(i + 1) * TILE, :]
        row_sums(grad * grad * inv_col, groups, i)
    v_copy = []
    for q in range(1, n):
        copy = pltpu.make_async_remote_copy(
            src_ref=rv.at[0], dst_ref=rv.at[q], send_sem=v_send.at[q], recv_sem=v_recv.at[q],
            device_id=(flip(me, q), mp), device_id_type=MESH)
        copy.start()
        v_copy.append(copy)
    context_grad(last[len(last) // 2:], False, True)
    for copy in v_copy:
        copy.wait_recv()
    sums = [rv[q] for q in range(n)]
    while len(sums) > 1:
        sums = [sums[k] + sums[k + 1] for k in range(0, len(sums), 2)]
    row_new = decay_rate * row_ref[...] + (1.0 - decay_rate) * (sums[0][:groups] / width)
    rown_ref[...] = row_new
    part = jnp.sum(jnp.sum(sums[0][groups:] / row_new, axis=0, keepdims=True), axis=1, keepdims=True)
    sx[0] = jnp.broadcast_to(part, (8, LANES))
    s_copy = pltpu.make_async_remote_copy(
        src_ref=sx.at[0], dst_ref=sx.at[1], send_sem=p_send.at[1], recv_sem=p_recv.at[1],
        device_id=(me, other), device_id_type=MESH)
    s_copy.start()
    root_row = 1.0 / jnp.sqrt(row_new)
    root_col = 1.0 / jnp.sqrt(col_new)
    s_copy.wait_recv()
    rms = jnp.sqrt((sx[0, 0:1, :] + sx[1, 0:1, :]) / (2.0 * heads * width))
    root_row = root_row / jnp.maximum(1.0, rms)
    for k in range(groups):
        factor = jnp.broadcast_to(root_row[k:k + 1, :], (LANES, LANES)).T
        factor = jnp.concatenate([factor] * (cols // LANES), axis=1)
        rows = slice(k * LANES, (k + 1) * LANES)
        up_ref[rows, :] = kept[0, rows, :] * factor * root_col

    for r in order[max(n - WINDOW, 0):]:
        x_copy[r].wait_send()
    for copy in w_copies:
        copy.wait_send()
    for r in range(1, n):
        r_copy[r].wait_send()
    col_copy.wait_send()
    for copy in v_copy:
        copy.wait_send()
    s_copy.wait_send()


def fused(n, context, cotangent, lengths, weight, row_stat, col_stat):
    t, width = cotangent.shape
    heads, cols = weight.shape
    target_len = t // lengths.shape[0]
    groups = heads // LANES
    inside = jnp.arange(target_len, dtype=jnp.int32)[None, :] < lengths[:, None]
    mask = jnp.broadcast_to(inside[:, :, None], (lengths.shape[0], target_len, LANES))
    mask = mask.astype(jnp.bfloat16).reshape(t, LANES)
    vmem = pl.BlockSpec(memory_space=pltpu.VMEM)
    dma = pltpu.SemaphoreType.DMA
    flops = 4 * 2 * t * heads * width
    out = pl.pallas_call(
        functools.partial(kernel, n),
        out_shape=(
            jax.ShapeDtypeStruct((2 * t, heads), jnp.bfloat16),
            jax.ShapeDtypeStruct((heads, cols), jnp.float32),
            jax.ShapeDtypeStruct((groups, LANES), jnp.float32),
            jax.ShapeDtypeStruct((1, cols), jnp.float32),
        ),
        in_specs=[vmem] * 6,
        out_specs=(vmem,) * 4,
        scratch_shapes=[
            pltpu.VMEM((heads, 2 * t), jnp.bfloat16),
            pltpu.VMEM((n, 2 * t, cols), jnp.bfloat16),
            pltpu.VMEM((n, heads, cols), jnp.bfloat16),
            pltpu.VMEM((n - 1, heads, cols), jnp.bfloat16),
            pltpu.VMEM((n - 1, heads, cols), jnp.bfloat16),
            pltpu.VMEM((n // 2, heads, cols), jnp.float32),
            pltpu.VMEM((2 * t, heads), jnp.float32),
            pltpu.VMEM((n, 2 * groups, LANES), jnp.float32),
            pltpu.VMEM((2, 8, cols), jnp.float32),
            pltpu.VMEM((2, 8, LANES), jnp.float32),
            dma((n,)), dma((n,)), dma((n,)), dma((n,)), dma((n,)), dma((n,)), dma((n,)), dma((n,)),
            dma((2,)), dma((2,)),
        ],
        compiler_params=pltpu.CompilerParams(
            collective_id=0, has_side_effects=True, vmem_limit_bytes=60 * 1024 * 1024
        ),
        cost_estimate=pl.CostEstimate(flops=flops, bytes_accessed=10 * t * width, transcendentals=0),
    )(mask, cotangent, context, weight, row_stat.reshape(groups, LANES), col_stat.reshape(1, cols))
    context_grad, update, row_new, col_new = out
    return context_grad, update, row_new.reshape(heads), col_new.reshape(cols)


def plain(context, cotangent, lengths, weight, row_stat, col_stat):
    data_groups = lax.axis_size("dp")
    seq_here = lengths.shape[0]
    target_len = cotangent.shape[0] // seq_here
    model_width = cotangent.shape[1]
    position = jnp.arange(target_len, dtype=jnp.int32)
    inside = position[None, :] < lengths[:, None]
    shaped = cotangent.reshape(seq_here, target_len, model_width)
    masked = jnp.where(inside[:, :, None], shaped, jnp.zeros((), cotangent.dtype)).reshape(
        -1, model_width
    )
    weight_b = weight.astype(jnp.bfloat16)
    head_cols = context.shape[1]
    gathered = lax.all_gather(masked, "mp", axis=0, tiled=True)
    back_ctx = lax.dot_general(
        gathered,
        lax.all_gather(weight_b, "dp", axis=1, tiled=True),
        (((1,), (1,)), ((), ())),
        preferred_element_type=jnp.float32,
    )
    grad_term = lax.dot_general(
        context, gathered, (((0,), (0,)), ((), ())), preferred_element_type=jnp.float32
    )
    context_grad = back_ctx.astype(jnp.bfloat16)
    grad = lax.psum_scatter(grad_term, "dp", scatter_dimension=1, tiled=True) / data_groups
    square = grad * grad + square_eps
    inner_total = head_cols * lax.axis_size("mp")
    row_all = lax.psum(jnp.sum(square, axis=1), "dp")
    row_new = decay_rate * row_stat + (1.0 - decay_rate) * (row_all / model_width)
    col_all = lax.psum(jnp.sum(square, axis=0), "mp")
    col_new = decay_rate * col_stat + (1.0 - decay_rate) * (col_all / inner_total)
    raw_update = grad / jnp.sqrt(row_new[:, None] * col_new[None, :])
    square_sum = lax.psum(jnp.sum(raw_update * raw_update), ("dp", "mp"))
    update_rms = jnp.sqrt(square_sum / (inner_total * model_width))
    update = raw_update / jnp.maximum(1.0, update_rms)
    return (context_grad, update, row_new, col_new)


def per_device(context, cotangent, lengths, weight, row_stat, col_stat):
    n = lax.axis_size("dp")
    heads, cols = weight.shape
    tokens = 2 * cotangent.shape[0]
    pairs = lax.axis_size("mp") == 2 and n >= 8 and n & (n - 1) == 0
    whole_tiles = heads % (8 * LANES) == 0 and cols % LANES == 0 and tokens % TILE == 0
    if pairs and whole_tiles:
        return fused(n, context, cotangent, lengths, weight, row_stat, col_stat)
    return plain(context, cotangent, lengths, weight, row_stat, col_stat)


def solution(mesh):
    in_specs = (
        P("dp", "mp"),
        P(("dp", "mp"), None),
        P(("dp", "mp")),
        P("mp", "dp"),
        P("mp"),
        P("dp"),
    )
    out_specs = (P("dp", "mp"), P("mp", "dp"), P("mp"), P("dp"))
    return jax.shard_map(
        per_device, mesh=mesh, in_specs=in_specs, out_specs=out_specs, check_vma=False
    )
```

```python
import functools
import jax
import jax.numpy as jnp
from jax import lax
from jax.experimental import pallas as pl
from jax.experimental.pallas import tpu as pltpu
from jax.sharding import PartitionSpec as P

decay_rate = 0.9
square_eps = 1e-30
LANES = 128
TILE = 256
WINDOW = 4
MESH = pl.DeviceIdType.MESH


def low_bit(r, n):
    return r & -r if r else n


def flip(me, r):
    out = me
    bit = 1
    while bit <= r:
        if r & bit:
            out = out + bit * (1 - 2 * (lax.rem(lax.div(me, bit), 2)))
        bit *= 2
    return out


def schedule(n):
    half = n // 2
    first = list(range(n - 2, half - 1, -2))
    second = sorted(range(0, half, 2), key=lambda r: (low_bit(r, n), -r))
    order = [b for r in first + second for b in (r + 1, r)]
    pos = {r: k for k, r in enumerate(order)}
    after = {}
    for r in sorted(range(2, n, 2), key=lambda r: low_bit(r, n)):
        when, bit = pos[r], 2
        while bit < low_bit(r, n):
            when = max(when, after[r + bit] + 3)
            bit *= 2
        after[r] = min(when, n - 2)
    return order, after


def weight_routes(n):
    bits = [1 << k for k in range(n.bit_length() - 2, 0, -1)]
    return bits + [1], bits[-1:] + bits[:-1] + [1]


def onward(route, r):
    used = [k for k, bit in enumerate(route) if r & bit]
    return route[used[-1] + 1:] if used else route


def weight_arrivals(n):
    pieces = [(r, h) for r in range(2, n, 2) for h in range(2)]
    return sorted(pieces, key=lambda p: (bin(p[0]).count("1"), len(onward(weight_routes(n)[p[1]], p[0])) * -1, p[1]))


def kernel(n, len_ref, cot_ref, ctx_ref, w_ref, row_ref, col_ref,
           cg_ref, up_ref, rown_ref, coln_ref,
           mask_ref, ctx_v, w_v, ctx_t, g_all, w_all, inbox, outbox, kept, cg_acc, rv, cx, sx,
           x_send, x_recv, w_send, w_recv, r_send, r_recv, v_send, v_recv, p_send, p_recv,
           b_sem, i_sem):
    me, mp = lax.axis_index("dp"), lax.axis_index("mp")
    other = 1 - mp
    t, width = cot_ref.shape
    heads, cols = w_ref.shape
    groups = heads // LANES
    own_rows = pl.ds(pl.multiple_of(mp * t, t), t)

    barrier = pltpu.get_barrier_semaphore()
    for q in range(1, n):
        pl.semaphore_signal(barrier, inc=1, device_id=(flip(me, q), mp), device_id_type=MESH)
    pl.semaphore_signal(barrier, inc=1, device_id=(me, other), device_id_type=MESH)

    order, after = schedule(n)

    block_in = {}
    for r in order:
        columns = pl.ds(pl.multiple_of(flip(me, r) * cols, cols), cols)
        block_in[r] = pltpu.make_async_copy(
            cot_ref.at[:, columns], g_all.at[r, own_rows, :], b_sem.at[r])
    w_in = pltpu.make_async_copy(w_ref, w_v, i_sem.at[0])
    ctx_in = pltpu.make_async_copy(ctx_ref, ctx_v, i_sem.at[1])
    for r in order[:WINDOW]:
        block_in[r].start()
    w_in.start()
    for r in order[WINDOW:]:
        block_in[r].start()
    ctx_in.start()

    seqs = len_ref.shape[0]
    slots = t // seqs
    position = lax.broadcasted_iota(jnp.int32, (slots, LANES), 0)
    for q in range(seqs):
        inside = jnp.where(position < len_ref[q], 1.0, 0.0)
        mask_ref[q * slots:(q + 1) * slots, :] = inside.astype(jnp.bfloat16)

    def mask_block(r):
        block_in[r].wait()
        m = mask_ref[...]
        m = jnp.concatenate([m] * (cols // LANES), axis=1)
        g_all[r, own_rows, :] = g_all[r, own_rows, :] * m

    mask_block(order[0])
    pl.semaphore_wait(barrier, n)

    x_copy = {}
    for r in order:
        x_copy[r] = pltpu.make_async_remote_copy(
            src_ref=g_all.at[r, own_rows, :], dst_ref=g_all.at[r, own_rows, :],
            send_sem=x_send.at[r], recv_sem=x_recv.at[r],
            device_id=(me, other), device_id_type=MESH)
    x_in = {
        r: pltpu.make_async_remote_copy(
            src_ref=g_all.at[r, own_rows, :],
            dst_ref=g_all.at[r, pl.ds(pl.multiple_of(other * t, t), t), :],
            send_sem=x_send.at[r], recv_sem=x_recv.at[r],
            device_id=(me, other), device_id_type=MESH)
        for r in order
    }
    for r in order[:WINDOW]:
        if r != order[0]:
            mask_block(r)
        x_copy[r].start()
    w_in.wait()
    w_all[0] = w_v[...].astype(jnp.bfloat16)

    w_copies = []
    cut = heads * 5 // 8 // LANES * LANES
    parts = (slice(0, cut), slice(cut, heads))

    def weight_send(r, h):
        for bit in onward(weight_routes(n)[h], r):
            copy = pltpu.make_async_remote_copy(
                src_ref=w_all.at[r, parts[h], :], dst_ref=w_all.at[r ^ bit, parts[h], :],
                send_sem=w_send.at[len(w_copies)], recv_sem=w_recv.at[r ^ bit, h],
                device_id=(flip(me, bit), mp), device_id_type=MESH)
            copy.start()
            w_copies.append(copy)

    w_seen = {(0, 0), (0, 1)}

    def weight_wait(r, h):
        if (r, h) in w_seen:
            return
        w_seen.add((r, h))
        pltpu.make_async_remote_copy(
            src_ref=w_all.at[0, parts[h], :], dst_ref=w_all.at[r, parts[h], :],
            send_sem=w_send.at[0], recv_sem=w_recv.at[r, h],
            device_id=(flip(me, 1), mp), device_id_type=MESH).wait_recv()

    weight_send(0, 0)
    weight_send(0, 1)
    for r in order[WINDOW:]:
        mask_block(r)

    tokens = 2 * t
    ctx_in.wait()
    for i in range(tokens // TILE):
        for j in range(heads // TILE):
            ctx_t[j * TILE:(j + 1) * TILE, i * TILE:(i + 1) * TILE] = ctx_v[
                i * TILE:(i + 1) * TILE, j * TILE:(j + 1) * TILE].T

    def reduce_copy(r):
        return pltpu.make_async_remote_copy(
            src_ref=outbox.at[r - 1], dst_ref=inbox.at[r - 1],
            send_sem=r_send.at[r], recv_sem=r_recv.at[r],
            device_id=(flip(me, low_bit(r, n)), mp), device_id_type=MESH)

    r_copy = {r: reduce_copy(r) for r in range(1, n)}

    def weight_grad(r):
        @pl.loop(0, heads // TILE)
        def _(i):
            rows = pl.ds(pl.multiple_of(i * TILE, TILE), TILE)
            term = jnp.dot(ctx_t[rows, :], g_all[r], preferred_element_type=jnp.float32)
            if r % 2:
                outbox[r - 1, rows, :] = term.astype(jnp.bfloat16)
            else:
                kept[r // 2, rows, :] = term
        if r % 2:
            r_copy[r].start()

    def incoming(r):
        out, bit = [], 1
        while bit < low_bit(r, n):
            out.append(r + bit)
            bit *= 2
        return out

    def pass_on(r):
        for q in incoming(r):
            r_copy[q].wait_recv()

        @pl.loop(0, heads // TILE)
        def _(i):
            rows = pl.ds(pl.multiple_of(i * TILE, TILE), TILE)
            total = kept[r // 2, rows, :]
            for q in incoming(r):
                total = total + inbox[q - 1, rows, :].astype(jnp.float32)
            outbox[r - 1, rows, :] = total.astype(jnp.bfloat16)
        r_copy[r].start()

    def context_grad(blocks, first, last):
        @pl.loop(0, tokens // TILE)
        def _(i):
            rows = pl.ds(pl.multiple_of(i * TILE, TILE), TILE)
            total = None if first else cg_acc[rows, :]
            for r in blocks:
                term = lax.dot_general(g_all[r, rows, :], w_all[r], (((1,), (1,)), ((), ())),
                                       preferred_element_type=jnp.float32)
                total = term if total is None else total + term
            if last:
                cg_ref[rows, :] = total.astype(jnp.bfloat16)
            else:
                cg_acc[rows, :] = total

    arrivals = weight_arrivals(n)
    w_step = {}
    for k, piece in enumerate(arrivals):
        w_step.setdefault(1 + k * (n // 2 - 1) // len(arrivals), []).append(piece)
    quarter = n // 4
    cg_step = {n // 2 + 1: 0, n // 2 + 3: 1, 3 * n // 4 + 1: 2}

    for k, r in enumerate(order):
        x_in[r].wait_recv()
        if k + WINDOW < n:
            x_copy[r].wait_send()
            x_copy[order[k + WINDOW]].start()
        weight_grad(r)
        for q in w_step.get(k, []):
            weight_wait(*q)
            weight_send(*q)
        for q in order:
            if after.get(q) == k:
                pass_on(q)
        if k in cg_step:
            blocks = order[cg_step[k] * quarter:(cg_step[k] + 1) * quarter]
            for q in blocks:
                weight_wait(q, 0)
                weight_wait(q, 1)
            context_grad(blocks, cg_step[k] == 0, False)

    for q in incoming(0):
        r_copy[q].wait_recv()
    col_part = jnp.zeros((1, cols), jnp.float32)

    def row_sums(values, base, i):
        folded = values[:, :LANES]
        for c in range(LANES, cols, LANES):
            folded = folded + values[:, c:c + LANES]
        line = jnp.sum(folded.T, axis=0, keepdims=True)
        for c in range(TILE // LANES):
            at = base + i * (TILE // LANES) + c
            rv[0, at:at + 1, :] = line[:, c * LANES:(c + 1) * LANES]

    for i in range(heads // TILE):
        rows = slice(i * TILE, (i + 1) * TILE)
        total = kept[0, rows, :]
        for q in incoming(0):
            total = total + inbox[q - 1, rows, :].astype(jnp.float32)
        grad = total / n
        kept[0, rows, :] = grad
        square = grad * grad + square_eps
        col_part = col_part + jnp.sum(square, axis=0, keepdims=True)
        row_sums(square, 0, i)
    cx[0] = jnp.broadcast_to(col_part, (8, cols))
    col_copy = pltpu.make_async_remote_copy(
        src_ref=cx.at[0], dst_ref=cx.at[1], send_sem=p_send.at[0], recv_sem=p_recv.at[0],
        device_id=(me, other), device_id_type=MESH)
    col_copy.start()
    last = order[3 * quarter:]
    for q in last:
        weight_wait(q, 0)
        weight_wait(q, 1)
    context_grad(last[:len(last) // 2], False, False)
    col_copy.wait_recv()
    col_new = decay_rate * col_ref[...] + (1.0 - decay_rate) * (
        (cx[0, 0:1, :] + cx[1, 0:1, :]) / (2 * heads))
    coln_ref[...] = col_new
    inv_col = 1.0 / col_new
    for i in range(heads // TILE):
        grad = kept[0, i * TILE:(i + 1) * TILE, :]
        row_sums(grad * grad * inv_col, groups, i)
    v_copy = []
    for q in range(1, n):
        copy = pltpu.make_async_remote_copy(
            src_ref=rv.at[0], dst_ref=rv.at[q], send_sem=v_send.at[q], recv_sem=v_recv.at[q],
            device_id=(flip(me, q), mp), device_id_type=MESH)
        copy.start()
        v_copy.append(copy)
    context_grad(last[len(last) // 2:], False, True)
    for copy in v_copy:
        copy.wait_recv()
    sums = [rv[q] for q in range(n)]
    while len(sums) > 1:
        sums = [sums[k] + sums[k + 1] for k in range(0, len(sums), 2)]
    row_new = decay_rate * row_ref[...] + (1.0 - decay_rate) * (sums[0][:groups] / width)
    rown_ref[...] = row_new
    part = jnp.sum(jnp.sum(sums[0][groups:] / row_new, axis=0, keepdims=True), axis=1, keepdims=True)
    sx[0] = jnp.broadcast_to(part, (8, LANES))
    s_copy = pltpu.make_async_remote_copy(
        src_ref=sx.at[0], dst_ref=sx.at[1], send_sem=p_send.at[1], recv_sem=p_recv.at[1],
        device_id=(me, other), device_id_type=MESH)
    s_copy.start()
    root_row = 1.0 / jnp.sqrt(row_new)
    root_col = 1.0 / jnp.sqrt(col_new)
    s_copy.wait_recv()
    rms = jnp.sqrt((sx[0, 0:1, :] + sx[1, 0:1, :]) / (2.0 * heads * width))
    root_row = root_row / jnp.maximum(1.0, rms)
    for k in range(groups):
        factor = jnp.broadcast_to(root_row[k:k + 1, :], (LANES, LANES)).T
        factor = jnp.concatenate([factor] * (cols // LANES), axis=1)
        rows = slice(k * LANES, (k + 1) * LANES)
        up_ref[rows, :] = kept[0, rows, :] * factor * root_col

    for r in order[max(n - WINDOW, 0):]:
        x_copy[r].wait_send()
    for copy in w_copies:
        copy.wait_send()
    for r in range(1, n):
        r_copy[r].wait_send()
    col_copy.wait_send()
    for copy in v_copy:
        copy.wait_send()
    s_copy.wait_send()


def hand_on(*arrays):
    steps = 4

    def body(*refs):
        for src, dst in zip(refs[:len(arrays)], refs[len(arrays):]):
            dst[...] = src[...]

    def spec(a):
        if a.shape[0] % (16 * steps) == 0:
            return pl.BlockSpec((a.shape[0] // steps, a.shape[1]), lambda i: (i, 0))
        return pl.BlockSpec(a.shape, lambda i: (0, 0))

    return pl.pallas_call(
        body, grid=(steps,), in_specs=[spec(a) for a in arrays], out_specs=[spec(a) for a in arrays],
        out_shape=[jax.ShapeDtypeStruct(a.shape, a.dtype) for a in arrays],
    )(*arrays)


def fused(n, context, cotangent, lengths, weight, row_stat, col_stat):
    t, width = cotangent.shape
    heads, cols = weight.shape
    groups = heads // LANES
    vmem = pl.BlockSpec(memory_space=pltpu.VMEM)
    dma = pltpu.SemaphoreType.DMA
    flops = 4 * 2 * t * heads * width
    out = pl.pallas_call(
        functools.partial(kernel, n),
        out_shape=(
            jax.ShapeDtypeStruct((2 * t, heads), jnp.bfloat16),
            jax.ShapeDtypeStruct((heads, cols), jnp.float32),
            jax.ShapeDtypeStruct((groups, LANES), jnp.float32),
            jax.ShapeDtypeStruct((1, cols), jnp.float32),
        ),
        in_specs=[pl.BlockSpec(memory_space=pltpu.SMEM)] + [pl.BlockSpec(memory_space=pl.ANY)] * 3 + [vmem] * 2,
        out_specs=(vmem,) * 4,
        scratch_shapes=[
            pltpu.VMEM((t, LANES), jnp.bfloat16),
            pltpu.VMEM((2 * t, heads), jnp.bfloat16),
            pltpu.VMEM((heads, cols), jnp.float32),
            pltpu.VMEM((heads, 2 * t), jnp.bfloat16),
            pltpu.VMEM((n, 2 * t, cols), jnp.bfloat16),
            pltpu.VMEM((n, heads, cols), jnp.bfloat16),
            pltpu.VMEM((n - 1, heads, cols), jnp.bfloat16),
            pltpu.VMEM((n - 1, heads, cols), jnp.bfloat16),
            pltpu.VMEM((n // 2, heads, cols), jnp.float32),
            pltpu.VMEM((2 * t, heads), jnp.float32),
            pltpu.VMEM((n, 2 * groups, LANES), jnp.float32),
            pltpu.VMEM((2, 8, cols), jnp.float32),
            pltpu.VMEM((2, 8, LANES), jnp.float32),
            dma((n,)), dma((n,)), dma((2 * n,)), dma((n, 2)), dma((n,)), dma((n,)), dma((n,)), dma((n,)),
            dma((2,)), dma((2,)), dma((n,)), dma((2,)),
        ],
        compiler_params=pltpu.CompilerParams(
            collective_id=0, has_side_effects=True, vmem_limit_bytes=60 * 1024 * 1024
        ),
        cost_estimate=pl.CostEstimate(flops=flops, bytes_accessed=10 * t * width, transcendentals=0),
    )(lengths, cotangent, context, weight, row_stat.reshape(groups, LANES), col_stat.reshape(1, cols))
    context_grad, update, row_new, col_new = hand_on(*out)
    return context_grad, update, row_new.reshape(heads), col_new.reshape(cols)


def plain(context, cotangent, lengths, weight, row_stat, col_stat):
    data_groups = lax.axis_size("dp")
    seq_here = lengths.shape[0]
    target_len = cotangent.shape[0] // seq_here
    model_width = cotangent.shape[1]
    position = jnp.arange(target_len, dtype=jnp.int32)
    inside = position[None, :] < lengths[:, None]
    shaped = cotangent.reshape(seq_here, target_len, model_width)
    masked = jnp.where(inside[:, :, None], shaped, jnp.zeros((), cotangent.dtype)).reshape(
        -1, model_width
    )
    weight_b = weight.astype(jnp.bfloat16)
    head_cols = context.shape[1]
    gathered = lax.all_gather(masked, "mp", axis=0, tiled=True)
    back_ctx = lax.dot_general(
        gathered,
        lax.all_gather(weight_b, "dp", axis=1, tiled=True),
        (((1,), (1,)), ((), ())),
        preferred_element_type=jnp.float32,
    )
    grad_term = lax.dot_general(
        context, gathered, (((0,), (0,)), ((), ())), preferred_element_type=jnp.float32
    )
    context_grad = back_ctx.astype(jnp.bfloat16)
    grad = lax.psum_scatter(grad_term, "dp", scatter_dimension=1, tiled=True) / data_groups
    square = grad * grad + square_eps
    inner_total = head_cols * lax.axis_size("mp")
    row_all = lax.psum(jnp.sum(square, axis=1), "dp")
    row_new = decay_rate * row_stat + (1.0 - decay_rate) * (row_all / model_width)
    col_all = lax.psum(jnp.sum(square, axis=0), "mp")
    col_new = decay_rate * col_stat + (1.0 - decay_rate) * (col_all / inner_total)
    raw_update = grad / jnp.sqrt(row_new[:, None] * col_new[None, :])
    square_sum = lax.psum(jnp.sum(raw_update * raw_update), ("dp", "mp"))
    update_rms = jnp.sqrt(square_sum / (inner_total * model_width))
    update = raw_update / jnp.maximum(1.0, update_rms)
    return (context_grad, update, row_new, col_new)


def per_device(context, cotangent, lengths, weight, row_stat, col_stat):
    n = lax.axis_size("dp")
    heads, cols = weight.shape
    tokens = 2 * cotangent.shape[0]
    pairs = lax.axis_size("mp") == 2 and n >= 8 and n & (n - 1) == 0
    whole_tiles = heads % (8 * LANES) == 0 and cols % LANES == 0 and tokens % TILE == 0
    if pairs and whole_tiles:
        return fused(n, context, cotangent, lengths, weight, row_stat, col_stat)
    return plain(context, cotangent, lengths, weight, row_stat, col_stat)


def solution(mesh):
    in_specs = (
        P("dp", "mp"),
        P(("dp", "mp"), None),
        P(("dp", "mp")),
        P("mp", "dp"),
        P("mp"),
        P("dp"),
    )
    out_specs = (P("dp", "mp"), P("mp", "dp"), P("mp"), P("dp"))
    return jax.shard_map(
        per_device, mesh=mesh, in_specs=in_specs, out_specs=out_specs, check_vma=False
    )
```

```python
import functools
import jax
import jax.numpy as jnp
from jax import lax
from jax.experimental import pallas as pl
from jax.experimental.pallas import tpu as pltpu
from jax.sharding import PartitionSpec as P

decay_rate = 0.9
square_eps = 1e-30
LANES = 128
TILE = 256
WINDOW = 4
MESH = pl.DeviceIdType.MESH


def low_bit(r, n):
    return r & -r if r else n


def flip(me, r):
    out = me
    bit = 1
    while bit <= r:
        if r & bit:
            out = out + bit * (1 - 2 * (lax.rem(lax.div(me, bit), 2)))
        bit *= 2
    return out


def schedule(n):
    half = n // 2
    first = list(range(n - 2, half - 1, -2))
    second = sorted(range(0, half, 2), key=lambda r: (low_bit(r, n), -r))
    order = [b for r in first + second for b in (r + 1, r)]
    pos = {r: k for k, r in enumerate(order)}
    after = {}
    for r in sorted(range(2, n, 2), key=lambda r: low_bit(r, n)):
        when, bit = pos[r], 2
        while bit < low_bit(r, n):
            when = max(when, after[r + bit] + 3)
            bit *= 2
        after[r] = min(when, n - 2)
    return order, after


def weight_routes(n):
    bits = [1 << k for k in range(n.bit_length() - 2, 0, -1)]
    return bits + [1], bits[-1:] + bits[:-1] + [1]


def onward(route, r):
    used = [k for k, bit in enumerate(route) if r & bit]
    return route[used[-1] + 1:] if used else route


def weight_arrivals(n):
    pieces = [(r, h) for r in range(2, n, 2) for h in range(2)]
    return sorted(pieces, key=lambda p: (bin(p[0]).count("1"), len(onward(weight_routes(n)[p[1]], p[0])) * -1, p[1]))


def kernel(n, len_ref, cot_ref, ctx_ref, w_ref, row_ref, col_ref,
           cg_ref, up_ref, rown_ref, coln_ref,
           cg_v, mask_ref, ctx_v, w_v, ctx_t, g_all, w_all, inbox, outbox, kept, cg_acc, rv, cx, sx,
           x_send, x_recv, w_send, w_recv, r_send, r_recv, v_send, v_recv, p_send, p_recv,
           b_sem, i_sem):
    me, mp = lax.axis_index("dp"), lax.axis_index("mp")
    other = 1 - mp
    t, width = cot_ref.shape
    heads, cols = w_ref.shape
    groups = heads // LANES
    own_rows = pl.ds(pl.multiple_of(mp * t, t), t)

    barrier = pltpu.get_barrier_semaphore()
    for q in range(1, n):
        pl.semaphore_signal(barrier, inc=1, device_id=(flip(me, q), mp), device_id_type=MESH)
    pl.semaphore_signal(barrier, inc=1, device_id=(me, other), device_id_type=MESH)

    order, after = schedule(n)

    block_in = {}
    for r in order:
        columns = pl.ds(pl.multiple_of(flip(me, r) * cols, cols), cols)
        block_in[r] = pltpu.make_async_copy(
            cot_ref.at[:, columns], g_all.at[r, own_rows, :], b_sem.at[r])
    w_in = pltpu.make_async_copy(w_ref, w_v, i_sem.at[0])
    ctx_in = pltpu.make_async_copy(ctx_ref, ctx_v, i_sem.at[1])
    for r in order[:WINDOW]:
        block_in[r].start()
    w_in.start()
    for r in order[WINDOW:]:
        block_in[r].start()
    ctx_in.start()

    seqs = len_ref.shape[0]
    slots = t // seqs
    position = lax.broadcasted_iota(jnp.int32, (slots, LANES), 0)
    for q in range(seqs):
        inside = jnp.where(position < len_ref[q], 1.0, 0.0)
        mask_ref[q * slots:(q + 1) * slots, :] = inside.astype(jnp.bfloat16)

    def mask_block(r):
        block_in[r].wait()
        m = mask_ref[...]
        m = jnp.concatenate([m] * (cols // LANES), axis=1)
        g_all[r, own_rows, :] = g_all[r, own_rows, :] * m

    mask_block(order[0])
    pl.semaphore_wait(barrier, n)

    x_copy = {}
    for r in order:
        x_copy[r] = pltpu.make_async_remote_copy(
            src_ref=g_all.at[r, own_rows, :], dst_ref=g_all.at[r, own_rows, :],
            send_sem=x_send.at[r], recv_sem=x_recv.at[r],
            device_id=(me, other), device_id_type=MESH)
    x_in = {
        r: pltpu.make_async_remote_copy(
            src_ref=g_all.at[r, own_rows, :],
            dst_ref=g_all.at[r, pl.ds(pl.multiple_of(other * t, t), t), :],
            send_sem=x_send.at[r], recv_sem=x_recv.at[r],
            device_id=(me, other), device_id_type=MESH)
        for r in order
    }
    for r in order[:WINDOW]:
        if r != order[0]:
            mask_block(r)
        x_copy[r].start()
    w_in.wait()
    w_all[0] = w_v[...].astype(jnp.bfloat16)

    w_copies = []
    cut = heads * 5 // 8 // LANES * LANES
    parts = (slice(0, cut), slice(cut, heads))

    def weight_send(r, h):
        for bit in onward(weight_routes(n)[h], r):
            copy = pltpu.make_async_remote_copy(
                src_ref=w_all.at[r, parts[h], :], dst_ref=w_all.at[r ^ bit, parts[h], :],
                send_sem=w_send.at[len(w_copies)], recv_sem=w_recv.at[r ^ bit, h],
                device_id=(flip(me, bit), mp), device_id_type=MESH)
            copy.start()
            w_copies.append(copy)

    w_seen = {(0, 0), (0, 1)}

    def weight_wait(r, h):
        if (r, h) in w_seen:
            return
        w_seen.add((r, h))
        pltpu.make_async_remote_copy(
            src_ref=w_all.at[0, parts[h], :], dst_ref=w_all.at[r, parts[h], :],
            send_sem=w_send.at[0], recv_sem=w_recv.at[r, h],
            device_id=(flip(me, 1), mp), device_id_type=MESH).wait_recv()

    weight_send(0, 0)
    weight_send(0, 1)
    for r in order[WINDOW:]:
        mask_block(r)

    tokens = 2 * t
    ctx_in.wait()
    for i in range(tokens // TILE):
        for j in range(heads // TILE):
            ctx_t[j * TILE:(j + 1) * TILE, i * TILE:(i + 1) * TILE] = ctx_v[
                i * TILE:(i + 1) * TILE, j * TILE:(j + 1) * TILE].T

    def reduce_copy(r):
        return pltpu.make_async_remote_copy(
            src_ref=outbox.at[r - 1], dst_ref=inbox.at[r - 1],
            send_sem=r_send.at[r], recv_sem=r_recv.at[r],
            device_id=(flip(me, low_bit(r, n)), mp), device_id_type=MESH)

    r_copy = {r: reduce_copy(r) for r in range(1, n)}

    def weight_grad(r):
        @pl.loop(0, heads // TILE)
        def _(i):
            rows = pl.ds(pl.multiple_of(i * TILE, TILE), TILE)
            term = jnp.dot(ctx_t[rows, :], g_all[r], preferred_element_type=jnp.float32)
            if r % 2:
                outbox[r - 1, rows, :] = term.astype(jnp.bfloat16)
            else:
                kept[r // 2, rows, :] = term
        if r % 2:
            r_copy[r].start()

    def incoming(r):
        out, bit = [], 1
        while bit < low_bit(r, n):
            out.append(r + bit)
            bit *= 2
        return out

    def pass_on(r):
        for q in incoming(r):
            r_copy[q].wait_recv()

        @pl.loop(0, heads // TILE)
        def _(i):
            rows = pl.ds(pl.multiple_of(i * TILE, TILE), TILE)
            total = kept[r // 2, rows, :]
            for q in incoming(r):
                total = total + inbox[q - 1, rows, :].astype(jnp.float32)
            outbox[r - 1, rows, :] = total.astype(jnp.bfloat16)
        r_copy[r].start()

    def context_grad(blocks, first, last):
        @pl.loop(0, tokens // TILE)
        def _(i):
            rows = pl.ds(pl.multiple_of(i * TILE, TILE), TILE)
            total = None if first else cg_acc[rows, :]
            for r in blocks:
                term = lax.dot_general(g_all[r, rows, :], w_all[r], (((1,), (1,)), ((), ())),
                                       preferred_element_type=jnp.float32)
                total = term if total is None else total + term
            if last:
                cg_v[rows, :] = total.astype(jnp.bfloat16)
            else:
                cg_acc[rows, :] = total

    arrivals = weight_arrivals(n)
    w_step = {}
    for k, piece in enumerate(arrivals):
        w_step.setdefault(1 + k * (n // 2 - 1) // len(arrivals), []).append(piece)
    quarter = n // 4
    cg_step = {n // 2 + 1: 0, n // 2 + 3: 1, 3 * n // 4 + 1: 2}

    for k, r in enumerate(order):
        x_in[r].wait_recv()
        if k + WINDOW < n:
            x_copy[r].wait_send()
            x_copy[order[k + WINDOW]].start()
        weight_grad(r)
        for q in w_step.get(k, []):
            weight_wait(*q)
            weight_send(*q)
        for q in order:
            if after.get(q) == k:
                pass_on(q)
        if k in cg_step:
            blocks = order[cg_step[k] * quarter:(cg_step[k] + 1) * quarter]
            for q in blocks:
                weight_wait(q, 0)
                weight_wait(q, 1)
            context_grad(blocks, cg_step[k] == 0, False)
        if k == n - 2:
            blocks = order[3 * quarter:n - 2]
            for q in blocks + order[n - 2:]:
                weight_wait(q, 0)
                weight_wait(q, 1)
            context_grad(blocks, False, False)

    for q in incoming(0):
        r_copy[q].wait_recv()
    col_part = jnp.zeros((1, cols), jnp.float32)

    def row_sums(values, base, i):
        folded = values[:, :LANES]
        for c in range(LANES, cols, LANES):
            folded = folded + values[:, c:c + LANES]
        line = jnp.sum(folded.T, axis=0, keepdims=True)
        for c in range(TILE // LANES):
            at = base + i * (TILE // LANES) + c
            rv[0, at:at + 1, :] = line[:, c * LANES:(c + 1) * LANES]

    for i in range(heads // TILE):
        rows = slice(i * TILE, (i + 1) * TILE)
        total = kept[0, rows, :]
        for q in incoming(0):
            total = total + inbox[q - 1, rows, :].astype(jnp.float32)
        grad = total / n
        kept[0, rows, :] = grad
        square = grad * grad + square_eps
        col_part = col_part + jnp.sum(square, axis=0, keepdims=True)
        row_sums(square, 0, i)
    cx[0] = jnp.broadcast_to(col_part, (8, cols))
    col_copy = pltpu.make_async_remote_copy(
        src_ref=cx.at[0], dst_ref=cx.at[1], send_sem=p_send.at[0], recv_sem=p_recv.at[0],
        device_id=(me, other), device_id_type=MESH)
    col_copy.start()
    last = order[n - 2:]
    context_grad(last[:1], False, False)
    col_copy.wait_recv()
    col_new = decay_rate * col_ref[...] + (1.0 - decay_rate) * (
        (cx[0, 0:1, :] + cx[1, 0:1, :]) / (2 * heads))
    coln_ref[...] = col_new
    inv_col = 1.0 / col_new
    for i in range(heads // TILE):
        grad = kept[0, i * TILE:(i + 1) * TILE, :]
        row_sums(grad * grad * inv_col, groups, i)
    v_copy = []
    for q in range(1, n):
        copy = pltpu.make_async_remote_copy(
            src_ref=rv.at[0], dst_ref=rv.at[q], send_sem=v_send.at[q], recv_sem=v_recv.at[q],
            device_id=(flip(me, q), mp), device_id_type=MESH)
        copy.start()
        v_copy.append(copy)
    context_grad(last[-1:], False, True)
    cg_out = pltpu.make_async_copy(cg_v, cg_ref, i_sem.at[2])
    cg_out.start()
    for copy in v_copy:
        copy.wait_recv()
    sums = [rv[q] for q in range(n)]
    while len(sums) > 1:
        sums = [sums[k] + sums[k + 1] for k in range(0, len(sums), 2)]
    row_new = decay_rate * row_ref[...] + (1.0 - decay_rate) * (sums[0][:groups] / width)
    rown_ref[...] = row_new
    part = jnp.sum(jnp.sum(sums[0][groups:] / row_new, axis=0, keepdims=True), axis=1, keepdims=True)
    sx[0] = jnp.broadcast_to(part, (8, LANES))
    s_copy = pltpu.make_async_remote_copy(
        src_ref=sx.at[0], dst_ref=sx.at[1], send_sem=p_send.at[1], recv_sem=p_recv.at[1],
        device_id=(me, other), device_id_type=MESH)
    s_copy.start()
    root_row = 1.0 / jnp.sqrt(row_new)
    root_col = 1.0 / jnp.sqrt(col_new)
    s_copy.wait_recv()
    rms = jnp.sqrt((sx[0, 0:1, :] + sx[1, 0:1, :]) / (2.0 * heads * width))
    root_row = root_row / jnp.maximum(1.0, rms)
    for k in range(groups):
        factor = jnp.broadcast_to(root_row[k:k + 1, :], (LANES, LANES)).T
        factor = jnp.concatenate([factor] * (cols // LANES), axis=1)
        rows = slice(k * LANES, (k + 1) * LANES)
        up_ref[rows, :] = kept[0, rows, :] * factor * root_col

    for r in order[max(n - WINDOW, 0):]:
        x_copy[r].wait_send()
    for copy in w_copies:
        copy.wait_send()
    for r in range(1, n):
        r_copy[r].wait_send()
    col_copy.wait_send()
    for copy in v_copy:
        copy.wait_send()
    s_copy.wait_send()
    cg_out.wait()


def hand_on(*arrays):
    pieces = []
    for k, a in enumerate(arrays):
        size = 128 if a.shape[0] % 128 == 0 else a.shape[0]
        pieces += [(k, slice(i, i + size)) for i in range(0, a.shape[0], size)]
    count = len(arrays)

    def body(*refs):
        src, dst, held = refs[:count], refs[count:2 * count], refs[2 * count:3 * count]
        sem_in, sem_out = refs[3 * count:]
        into = [pltpu.make_async_copy(src[k].at[rows, :], held[k].at[rows, :], sem_in.at[i])
                for i, (k, rows) in enumerate(pieces)]
        out = [pltpu.make_async_copy(held[k].at[rows, :], dst[k].at[rows, :], sem_out.at[i])
               for i, (k, rows) in enumerate(pieces)]
        for copy in into:
            copy.start()
        for first, second in zip(into, out):
            first.wait()
            second.start()
        for copy in out:
            copy.wait()

    anywhere = pl.BlockSpec(memory_space=pl.ANY)
    return pl.pallas_call(
        body, in_specs=[anywhere] * count, out_specs=[anywhere] * count,
        out_shape=[jax.ShapeDtypeStruct(a.shape, a.dtype) for a in arrays],
        scratch_shapes=[pltpu.VMEM(a.shape, a.dtype) for a in arrays]
        + [pltpu.SemaphoreType.DMA((len(pieces),)), pltpu.SemaphoreType.DMA((len(pieces),))],
        compiler_params=pltpu.CompilerParams(vmem_limit_bytes=60 * 1024 * 1024),
    )(*arrays)


def fused(n, context, cotangent, lengths, weight, row_stat, col_stat):
    t, width = cotangent.shape
    heads, cols = weight.shape
    groups = heads // LANES
    vmem = pl.BlockSpec(memory_space=pltpu.VMEM)
    dma = pltpu.SemaphoreType.DMA
    flops = 4 * 2 * t * heads * width
    out = pl.pallas_call(
        functools.partial(kernel, n),
        out_shape=(
            jax.ShapeDtypeStruct((2 * t, heads), jnp.bfloat16),
            jax.ShapeDtypeStruct((heads, cols), jnp.float32),
            jax.ShapeDtypeStruct((groups, LANES), jnp.float32),
            jax.ShapeDtypeStruct((1, cols), jnp.float32),
        ),
        in_specs=[pl.BlockSpec(memory_space=pltpu.SMEM)] + [pl.BlockSpec(memory_space=pl.ANY)] * 3 + [vmem] * 2,
        out_specs=(pl.BlockSpec(memory_space=pl.ANY),) + (vmem,) * 3,
        scratch_shapes=[
            pltpu.VMEM((2 * t, heads), jnp.bfloat16),
            pltpu.VMEM((t, LANES), jnp.bfloat16),
            pltpu.VMEM((2 * t, heads), jnp.bfloat16),
            pltpu.VMEM((heads, cols), jnp.float32),
            pltpu.VMEM((heads, 2 * t), jnp.bfloat16),
            pltpu.VMEM((n, 2 * t, cols), jnp.bfloat16),
            pltpu.VMEM((n, heads, cols), jnp.bfloat16),
            pltpu.VMEM((n - 1, heads, cols), jnp.bfloat16),
            pltpu.VMEM((n - 1, heads, cols), jnp.bfloat16),
            pltpu.VMEM((n // 2, heads, cols), jnp.float32),
            pltpu.VMEM((2 * t, heads), jnp.float32),
            pltpu.VMEM((n, 2 * groups, LANES), jnp.float32),
            pltpu.VMEM((2, 8, cols), jnp.float32),
            pltpu.VMEM((2, 8, LANES), jnp.float32),
            dma((n,)), dma((n,)), dma((2 * n,)), dma((n, 2)), dma((n,)), dma((n,)), dma((n,)), dma((n,)),
            dma((2,)), dma((2,)), dma((n,)), dma((3,)),
        ],
        compiler_params=pltpu.CompilerParams(
            collective_id=0, has_side_effects=True, vmem_limit_bytes=60 * 1024 * 1024
        ),
        cost_estimate=pl.CostEstimate(flops=flops, bytes_accessed=10 * t * width, transcendentals=0),
    )(lengths, cotangent, context, weight, row_stat.reshape(groups, LANES), col_stat.reshape(1, cols))
    context_grad, update, row_new, col_new = hand_on(*out)
    return context_grad, update, row_new.reshape(heads), col_new.reshape(cols)


def plain(context, cotangent, lengths, weight, row_stat, col_stat):
    data_groups = lax.axis_size("dp")
    seq_here = lengths.shape[0]
    target_len = cotangent.shape[0] // seq_here
    model_width = cotangent.shape[1]
    position = jnp.arange(target_len, dtype=jnp.int32)
    inside = position[None, :] < lengths[:, None]
    shaped = cotangent.reshape(seq_here, target_len, model_width)
    masked = jnp.where(inside[:, :, None], shaped, jnp.zeros((), cotangent.dtype)).reshape(
        -1, model_width
    )
    weight_b = weight.astype(jnp.bfloat16)
    head_cols = context.shape[1]
    gathered = lax.all_gather(masked, "mp", axis=0, tiled=True)
    back_ctx = lax.dot_general(
        gathered,
        lax.all_gather(weight_b, "dp", axis=1, tiled=True),
        (((1,), (1,)), ((), ())),
        preferred_element_type=jnp.float32,
    )
    grad_term = lax.dot_general(
        context, gathered, (((0,), (0,)), ((), ())), preferred_element_type=jnp.float32
    )
    context_grad = back_ctx.astype(jnp.bfloat16)
    grad = lax.psum_scatter(grad_term, "dp", scatter_dimension=1, tiled=True) / data_groups
    square = grad * grad + square_eps
    inner_total = head_cols * lax.axis_size("mp")
    row_all = lax.psum(jnp.sum(square, axis=1), "dp")
    row_new = decay_rate * row_stat + (1.0 - decay_rate) * (row_all / model_width)
    col_all = lax.psum(jnp.sum(square, axis=0), "mp")
    col_new = decay_rate * col_stat + (1.0 - decay_rate) * (col_all / inner_total)
    raw_update = grad / jnp.sqrt(row_new[:, None] * col_new[None, :])
    square_sum = lax.psum(jnp.sum(raw_update * raw_update), ("dp", "mp"))
    update_rms = jnp.sqrt(square_sum / (inner_total * model_width))
    update = raw_update / jnp.maximum(1.0, update_rms)
    return (context_grad, update, row_new, col_new)


def per_device(context, cotangent, lengths, weight, row_stat, col_stat):
    n = lax.axis_size("dp")
    heads, cols = weight.shape
    tokens = 2 * cotangent.shape[0]
    pairs = lax.axis_size("mp") == 2 and n >= 8 and n & (n - 1) == 0
    whole_tiles = heads % (8 * LANES) == 0 and cols % LANES == 0 and tokens % TILE == 0
    if pairs and whole_tiles:
        return fused(n, context, cotangent, lengths, weight, row_stat, col_stat)
    return plain(context, cotangent, lengths, weight, row_stat, col_stat)


def solution(mesh):
    in_specs = (
        P("dp", "mp"),
        P(("dp", "mp"), None),
        P(("dp", "mp")),
        P("mp", "dp"),
        P("mp"),
        P("dp"),
    )
    out_specs = (P("dp", "mp"), P("mp", "dp"), P("mp"), P("dp"))
    return jax.shard_map(
        per_device, mesh=mesh, in_specs=in_specs, out_specs=out_specs, check_vma=False
    )
```
